256 devices in a mesh: dp: 8 (over y, core), expert: 32 (over z, x).
Axes of the slice: x: 4, y: 4, z: 8, core: 2. Of those that a mesh axis runs over, the one named last changes fastest.
Arguments:
- tokens: bfloat16 [2048, 4096], P(('dp', 'expert')), may hold values from -6 to 6
- gate_values: bfloat16 [2048, 8], P(('dp', 'expert')), may hold values from 0.049804688 to 0.59765625
- expert_ids: int32 [2048, 8], P(('dp', 'expert')), may hold values from 0 to 63, all different within a row
- gate_weight: bfloat16 [64, 1536, 4096], P('expert', 'dp'), may hold values from -0.09375 to 0.09375
- up_weight: bfloat16 [64, 1536, 4096], P('expert', 'dp'), may hold values from -0.09375 to 0.09375
- down_weight: bfloat16 [64, 1536, 4096], P('expert', 'dp'), may hold values from -0.15625 to 0.15625
Outputs:
- mixed_out: bfloat16 [2048, 4096], P(('dp', 'expert'))
The draws below stay inside these ranges and needn't reach their ends.
All inputs are finite; a program needn't handle non-finite values.
Results may differ from the reference program's by a relative error of at most 0.019.
Values may be sent and summed in bfloat16 or wider, within the bound.
No kernel may reach another device: no remote copies, remote signals or barrier semaphores. Data moves between devices by JAX's collectives and lax.ppermute only.
A program may use at most 128 MiB of HBM per device.

```python
import math
import jax
import jax.numpy as jnp
from jax import lax

D = 4096
HID = 1536
TOP = 8
TOK_DEV = 8
EXPERTS = 64
CAP = 2
TOKENS = 2048
N_DP = 8


def shard_levels(rng, dims, split, least, high):
    gain = 1.0
    for position, parts in split:
        draws = jax.random.uniform(jax.random.fold_in(jax.random.fold_in(rng, 6), position), (parts,), jnp.float32, least / len(split), high / len(split))
        gain = gain * jnp.repeat(jnp.exp(draws), dims[position] // parts).reshape((-1,) + (1,) * (len(dims) - 1 - position))
    return gain


def choose_distinct(key, rows, amount, top, lift):
    order = jax.random.permutation(jax.random.fold_in(key, 1), amount)
    pull = order
    for power in range(3):
        pull = pull * pull // amount
    pull = pull * lift // amount
    tickets = jax.random.randint(jax.random.fold_in(key, 2), (rows, amount), 0, 4096) + pull
    sure = jax.random.permutation(jax.random.fold_in(key, 3), rows)[jnp.arange(amount) % rows]
    tickets = jnp.where(jnp.arange(rows)[:, None] == sure[None, :], 1 << 14, tickets)
    merit = tickets * amount + jnp.arange(amount)
    return lax.top_k(merit.astype(jnp.int32), top)[1].astype(jnp.int32)


def bell_draw(own_key, extent, scale, reach, shards=(), kind=jnp.bfloat16):
    result = scale * jax.random.normal(own_key, extent, jnp.float32)
    if shards:
        result = result * shard_levels(own_key, extent, shards, -0.22, 0.18)
    return jnp.clip(result, -reach, reach).astype(kind)


def setup_inputs(seed: int = 0) -> dict:
    key_of = jax.random.split(jax.random.key(seed), 7)
    return {
        "tokens": bell_draw(key_of[0], (TOKENS, D), 1.0, 6.0, ((0, 256),)),
        "gate_values": jnp.clip(jnp.exp(math.log(0.59765625) - 2.4849066 * jax.random.uniform(key_of[1], (TOKENS, TOP), jnp.float32) ** shard_levels(key_of[1], (TOKENS, TOP), ((0, 256),), -0.2, 0.2)), 0.049804688, 0.59765625).astype(jnp.bfloat16),
        "expert_ids": choose_distinct(key_of[2], TOKENS, EXPERTS, TOP, 1024),
        "gate_weight": bell_draw(key_of[3], (EXPERTS, HID, D), D ** -0.5, 0.09375, ((0, 32), (1, 8))),
        "up_weight": bell_draw(key_of[4], (EXPERTS, HID, D), D ** -0.5, 0.09375, ((0, 32), (1, 8))),
        "down_weight": bell_draw(key_of[5], (EXPERTS, HID, D), HID ** -0.5, 0.15625, ((0, 32), (1, 8))),
    }


def slot_ranks(choice_table, expert_count):
    onehot = (choice_table[:, :, None] == jnp.arange(expert_count, dtype=jnp.int32)[None, None, :]).astype(jnp.int32)
    before = jnp.cumsum(onehot, axis=1) - onehot
    return jnp.sum(before * onehot, axis=2)


def reference(tokens, gate_values, expert_ids, gate_weight, up_weight, down_weight):
    blocks = TOKENS // TOK_DEV
    choice_table = expert_ids.reshape(blocks, TOK_DEV * TOP)
    ranked = slot_ranks(choice_table, EXPERTS)
    keep_mask = ranked < CAP
    block_index = jnp.arange(blocks, dtype=jnp.int32)[:, None]
    total_slots = EXPERTS * blocks * CAP
    target = (choice_table * blocks + block_index) * CAP + ranked
    target = jnp.where(keep_mask, target, total_slots).reshape(-1).astype(jnp.int32)
    repeated = jnp.repeat(tokens, TOP, axis=0)
    dispatch = jnp.zeros((total_slots, D), jnp.bfloat16).at[target].set(repeated, mode="drop")
    dispatch = dispatch.reshape(EXPERTS, blocks * CAP, D)
    slice_width = HID // N_DP

    def one_expert(operands):
        rows_in, w_gate, w_up, w_down = operands
        gate_act = jnp.dot(rows_in, w_gate.T, preferred_element_type=jnp.float32)
        up_act = jnp.dot(rows_in, w_up.T, preferred_element_type=jnp.float32)
        hidden = (jax.nn.silu(gate_act) * up_act).astype(jnp.bfloat16)
        grouped = hidden.reshape(-1, N_DP, slice_width).astype(jnp.float32)
        pieces = jnp.einsum("rgh,ghd->grd", grouped, w_down.reshape(N_DP, slice_width, D).astype(jnp.float32))
        pieces = lax.optimization_barrier(pieces.astype(jnp.bfloat16)).astype(jnp.float32)
        return jnp.sum(pieces, axis=0)

    outputs = lax.map(one_expert, (dispatch, gate_weight, up_weight, down_weight))
    flat_out = outputs.reshape(total_slots, D)
    picked = flat_out[jnp.minimum(target, total_slots - 1)]
    weights_kept = jnp.where(keep_mask.reshape(-1), gate_values.reshape(-1).astype(jnp.float32), jnp.float32(0.0))
    mixed_out = jnp.sum((picked * weights_kept[:, None]).reshape(TOKENS, TOP, D), axis=1)
    return mixed_out.astype(jnp.bfloat16)
```

```python
import jax
import jax.numpy as jnp
from jax import lax
from jax.sharding import PartitionSpec as P


def slot_table(expert_ids, expert_count, capacity):
    rows, top_count = expert_ids.shape
    pairs = rows * top_count
    flat = expert_ids.reshape(pairs)
    earlier = jnp.arange(pairs)[None, :] < jnp.arange(pairs)[:, None]
    same = flat[:, None] == flat[None, :]
    ranked = jnp.sum((same & earlier).astype(jnp.int32), axis=1).reshape(rows, top_count)
    return jnp.where(ranked < capacity, expert_ids * capacity + ranked, -1)


def body(tokens, gate_values, expert_ids, gate_weight, up_weight, down_weight):
    dp_count = lax.axis_size("dp")
    column_count = lax.axis_size("expert")
    per_device = gate_weight.shape[0]
    expert_count = per_device * column_count
    token_rows, model_width = tokens.shape
    top_count = expert_ids.shape[1]
    capacity = max(2, (5 * token_rows * top_count + 4 * expert_count - 1) // (4 * expert_count))
    slots = expert_count * capacity

    slot = slot_table(expert_ids, expert_count, capacity)
    hit = slot[:, :, None] == jnp.arange(slots, dtype=jnp.int32)[None, None, :]
    chosen = jnp.sum(hit.astype(jnp.float32), axis=1).astype(jnp.bfloat16)
    weights = jnp.sum(
        jnp.where(hit, gate_values.astype(jnp.float32)[:, :, None], 0.0), axis=1
    ).astype(jnp.bfloat16)

    dispatch = jnp.einsum(
        "ts,td->sd", chosen, tokens, preferred_element_type=jnp.float32
    ).astype(jnp.bfloat16)
    dispatch = dispatch.reshape(column_count, per_device * capacity, model_width)
    arrived = lax.all_to_all(dispatch, "expert", split_axis=0, concat_axis=0, tiled=True)
    arrived = arrived.reshape(column_count, per_device, capacity, model_width)
    arrived = jnp.swapaxes(arrived, 0, 1).reshape(
        per_device, column_count * capacity, model_width
    )
    shared = lax.all_gather(arrived, "dp", axis=0, tiled=False)
    gate_act = jnp.einsum("glrd,lhd->glrh", shared, gate_weight, preferred_element_type=jnp.float32)
    up_act = jnp.einsum("glrd,lhd->glrh", shared, up_weight, preferred_element_type=jnp.float32)
    hidden = (jax.nn.silu(gate_act) * up_act).astype(jnp.bfloat16)
    pieces = jnp.einsum(
        "glrh,lhd->glrd", hidden, down_weight, preferred_element_type=jnp.float32
    ).astype(jnp.bfloat16)
    summed = lax.psum_scatter(
        pieces.reshape(dp_count * per_device * column_count * capacity, model_width),
        "dp",
        scatter_dimension=0,
        tiled=True,
    )
    summed = summed.reshape(per_device, column_count, capacity, model_width)
    summed = jnp.swapaxes(summed, 0, 1).reshape(
        column_count, per_device * capacity, model_width
    )
    returned = lax.all_to_all(summed, "expert", split_axis=0, concat_axis=0, tiled=True)
    rows_back = returned.reshape(slots, model_width)
    mixed_out = jnp.einsum("ts,sd->td", weights, rows_back, preferred_element_type=jnp.float32)
    return mixed_out.astype(jnp.bfloat16)


def solution(mesh):
    return jax.shard_map(
        body,
        mesh=mesh,
        in_specs=(
            P(("dp", "expert"), None),
            P(("dp", "expert"), None),
            P(("dp", "expert"), None),
            P("expert", "dp", None),
            P("expert", "dp", None),
            P("expert", "dp", None),
        ),
        out_specs=P(("dp", "expert"), None),
        check_vma=False,
    )
```

```python
import functools

import jax
import jax.numpy as jnp
from jax import lax
from jax.experimental import pallas as pl
from jax.experimental.pallas import tpu as pltpu
from jax.sharding import PartitionSpec as P


def slot_table(expert_ids, capacity):
    rows, top_count = expert_ids.shape
    pairs = rows * top_count
    flat = expert_ids.reshape(pairs)
    earlier = jnp.arange(pairs)[None, :] < jnp.arange(pairs)[:, None]
    same = flat[:, None] == flat[None, :]
    ranked = jnp.sum((same & earlier).astype(jnp.int32), axis=1).reshape(rows, top_count)
    return jnp.where(ranked < capacity, expert_ids * capacity + ranked, -1)


def expert_kernel(count, *refs):
    pieces, (gate_ref, up_ref, down_ref), outs = refs[:count], refs[count : count + 3], refs[count + 3 :]
    rows = jnp.concatenate([ref[...] for ref in pieces], axis=0)
    transposed = (((1,), (1,)), ((), ()))
    gate_act = lax.dot_general(rows, gate_ref[0], transposed, preferred_element_type=jnp.float32)
    up_act = lax.dot_general(rows, up_ref[0], transposed, preferred_element_type=jnp.float32)
    hidden = (gate_act / (1.0 + jnp.exp(-gate_act)) * up_act).astype(jnp.bfloat16)
    out = jnp.dot(hidden, down_ref[0], preferred_element_type=jnp.float32).astype(jnp.bfloat16)
    height = out.shape[0] // len(outs)
    for i, ref in enumerate(outs):
        ref[...] = out[i * height : (i + 1) * height]


def expert_rows(pieces, index, gate_weight, up_weight, down_weight):
    height, width = pieces[0].shape
    hidden = gate_weight.shape[1]
    count = len(pieces)
    weight = pl.BlockSpec((1, hidden, width), lambda i: (index, 0, 0))
    half = (count // 2 * height, width)
    return pl.pallas_call(
        functools.partial(expert_kernel, count),
        grid=(1,),
        in_specs=[pl.BlockSpec((height, width), lambda i: (0, 0))] * count + [weight] * 3,
        out_specs=[pl.BlockSpec(half, lambda i: (0, 0))] * 2,
        out_shape=[jax.ShapeDtypeStruct(half, jnp.bfloat16)] * 2,
        compiler_params=pltpu.CompilerParams(vmem_limit_bytes=56 * 1024 * 1024),
    )(*pieces, gate_weight, up_weight, down_weight)


def body(tokens, gate_values, expert_ids, gate_weight, up_weight, down_weight):
    dp_count = lax.axis_size("dp")
    ring = dp_count // 2
    column_count = lax.axis_size("expert")
    per_device = gate_weight.shape[0]
    expert_count = per_device * column_count
    token_rows, model_width = tokens.shape
    top_count = expert_ids.shape[1]
    capacity = max(2, (5 * token_rows * top_count + 4 * expert_count - 1) // (4 * expert_count))
    chunk_rows = column_count * capacity

    def along_ring(value, step):
        return lax.ppermute(
            value,
            "dp",
            [(2 * y + c, 2 * ((y + step) % ring) + c) for y in range(ring) for c in range(2)],
        )

    def across(value):
        return lax.ppermute(
            value, "dp", [(2 * y + c, 2 * y + 1 - c) for y in range(ring) for c in range(2)]
        )

    slot = slot_table(expert_ids, capacity)
    hit = slot[:, :, None] == jnp.arange(expert_count * capacity, dtype=jnp.int32)[None, None, :]
    chosen = jnp.sum(hit.astype(jnp.float32), axis=1).astype(jnp.bfloat16)
    weights = jnp.sum(
        jnp.where(hit, gate_values.astype(jnp.float32)[:, :, None], 0.0), axis=1
    ).astype(jnp.bfloat16)
    chosen = chosen.reshape(token_rows, column_count, per_device, capacity)
    weights = weights.reshape(token_rows, column_count, per_device, capacity)

    arrived = []
    for index in range(per_device):
        sent = jnp.einsum(
            "tcr,td->crd", chosen[:, :, index], tokens, preferred_element_type=jnp.float32
        ).astype(jnp.bfloat16)
        arrived.append(lax.all_to_all(sent, "expert", split_axis=0, concat_axis=0, tiled=True))

    sums = []
    for index in range(per_device):
        own = arrived[index].reshape(chunk_rows, model_width)
        near = [own] + [along_ring(own, -step) for step in range(1, ring)]
        far = [across(piece) for piece in near]
        kept, other = expert_rows(near + far, index, gate_weight, up_weight, down_weight)
        paired = across(other)
        pair = [
            (
                kept[k * chunk_rows : (k + 1) * chunk_rows].astype(jnp.float32)
                + paired[k * chunk_rows : (k + 1) * chunk_rows].astype(jnp.float32)
            ).astype(jnp.bfloat16)
            for k in range(ring)
        ]
        total = pair[0].astype(jnp.float32)
        for step in range(1, ring):
            total = total + along_ring(pair[step], step).astype(jnp.float32)
        sums.append(total.astype(jnp.bfloat16).reshape(column_count, capacity, model_width))

    mixed_out = jnp.zeros((token_rows, model_width), jnp.float32)
    for index in range(per_device):
        back = lax.all_to_all(sums[index], "expert", split_axis=0, concat_axis=0, tiled=True)
        mixed_out = mixed_out + jnp.einsum(
            "tcr,crd->td", weights[:, :, index], back, preferred_element_type=jnp.float32
        )
    return mixed_out.astype(jnp.bfloat16)


def solution(mesh):
    return jax.shard_map(
        body,
        mesh=mesh,
        in_specs=(
            P(("dp", "expert"), None),
            P(("dp", "expert"), None),
            P(("dp", "expert"), None),
            P("expert", "dp", None),
            P("expert", "dp", None),
            P("expert", "dp", None),
        ),
        out_specs=P(("dp", "expert"), None),
        check_vma=False,
    )
```

```python
import functools

import jax
import jax.numpy as jnp
from jax import lax
from jax.experimental import pallas as pl
from jax.experimental.pallas import tpu as pltpu
from jax.sharding import PartitionSpec as P


def slot_table(expert_ids, capacity):
    rows, top_count = expert_ids.shape
    pairs = rows * top_count
    flat = expert_ids.reshape(pairs)
    earlier = jnp.arange(pairs)[None, :] < jnp.arange(pairs)[:, None]
    same = flat[:, None] == flat[None, :]
    ranked = jnp.sum((same & earlier).astype(jnp.int32), axis=1).reshape(rows, top_count)
    return jnp.where(ranked < capacity, expert_ids * capacity + ranked, -1)


def expert_kernel(counts, *refs):
    total = sum(counts)
    pieces, (gate_ref, up_ref, down_ref), outs = refs[:total], refs[total : total + 3], refs[total + 3 :]
    transposed = (((1,), (1,)), ((), ()))
    width = down_ref.shape[2]
    step = min(512, width)
    for index, count in enumerate(counts):
        start = sum(counts[:index])

        @pl.when(pl.program_id(0) == index)
        def _(mine=slice(start, start + count)):
            rows = jnp.concatenate([ref[...] for ref in pieces[mine]], axis=0)
            gate_act = lax.dot_general(
                rows, gate_ref[0], transposed, preferred_element_type=jnp.float32
            )
            up_act = lax.dot_general(rows, up_ref[0], transposed, preferred_element_type=jnp.float32)
            hidden = (gate_act / (1.0 + jnp.exp(-gate_act)) * up_act).astype(jnp.bfloat16)
            for begin in range(0, width, step):
                columns = slice(begin, begin + step)
                out = jnp.dot(
                    hidden, down_ref[0, :, columns], preferred_element_type=jnp.float32
                ).astype(jnp.bfloat16)
                row = 0
                for ref in outs[mine]:
                    ref[:, columns] = out[row : row + ref.shape[0]]
                    row += ref.shape[0]


def expert_rows(pieces, gate_weight, up_weight, down_weight):
    flat = [piece for group in pieces for piece in group]
    rows = sum(piece.shape[0] for piece in flat)
    width = flat[0].shape[1]
    hidden = gate_weight.shape[1]
    whole = pl.BlockSpec(memory_space=pltpu.VMEM)
    weight = pl.BlockSpec((1, hidden, width), lambda i: (i, 0, 0))
    return pl.pallas_call(
        functools.partial(expert_kernel, [len(group) for group in pieces]),
        grid=(len(pieces),),
        in_specs=[whole] * len(flat) + [weight] * 3,
        out_specs=[whole] * len(flat),
        out_shape=[pltpu.VMEM(piece.shape, jnp.bfloat16) for piece in flat],
        cost_estimate=pl.CostEstimate(
            flops=6 * rows * hidden * width,
            bytes_accessed=6 * len(pieces) * hidden * width + 4 * rows * width,
            transcendentals=rows * hidden,
        ),
        compiler_params=pltpu.CompilerParams(vmem_limit_bytes=24 * 1024 * 1024),
    )(
        *(pltpu.with_memory_space_constraint(piece, pltpu.VMEM) for piece in flat),
        *(
            pltpu.with_memory_space_constraint(value, pltpu.HBM)
            for value in (gate_weight, up_weight, down_weight)
        ),
    )


def body(tokens, gate_values, expert_ids, gate_weight, up_weight, down_weight):
    dp_count = lax.axis_size("dp")
    ring = dp_count // 2
    assert ring == 4 and gate_weight.shape[0] == 2
    column_count = lax.axis_size("expert")
    per_device = gate_weight.shape[0]
    expert_count = per_device * column_count
    token_rows, model_width = tokens.shape
    top_count = expert_ids.shape[1]
    capacity = max(2, (5 * token_rows * top_count + 4 * expert_count - 1) // (4 * expert_count))
    chunk_rows = column_count * capacity

    def along_ring(value, step):
        return lax.ppermute(
            value,
            "dp",
            [(2 * y + c, 2 * ((y + step) % ring) + c) for y in range(ring) for c in range(2)],
        )

    def across(value):
        return lax.ppermute(
            value, "dp", [(2 * y + c, 2 * y + 1 - c) for y in range(ring) for c in range(2)]
        )

    slot = slot_table(expert_ids, capacity)
    hit = slot[:, :, None] == jnp.arange(expert_count * capacity, dtype=jnp.int32)[None, None, :]
    chosen = jnp.sum(hit.astype(jnp.float32), axis=1).astype(jnp.bfloat16)
    weights = jnp.sum(
        jnp.where(hit, gate_values.astype(jnp.float32)[:, :, None], 0.0), axis=1
    ).astype(jnp.bfloat16)

    sent = jnp.einsum("ts,td->sd", chosen, tokens, preferred_element_type=jnp.float32)
    sent = sent.astype(jnp.bfloat16).reshape(column_count, per_device * capacity, model_width)

    def columns(value):
        return lax.all_to_all(value, "expert", split_axis=0, concat_axis=0, tiled=True)

    def add(*values):
        total = values[0].astype(jnp.float32)
        for value in values[1:]:
            total = total + value.astype(jnp.float32)
        return total.astype(jnp.bfloat16)

    tie = lax.optimization_barrier

    def experts(first, second):
        return expert_rows((first, second), gate_weight, up_weight, down_weight)

    arrived = columns(sent).reshape(column_count, per_device, capacity, model_width)
    own0, own1 = (arrived[:, index].reshape(chunk_rows, model_width) for index in range(2))
    before0, after1, before1, after0 = tie(
        (along_ring(own0, 1), along_ring(own1, -1), along_ring(own1, 1), along_ring(own0, -1))
    )
    facing0, facing1 = along_ring(before0, 1), along_ring(after1, -1)

    a0, b0, fa0, fb0, a1, b1, fa1, fb1 = experts(
        (after0, before0, across(after0), across(before0)),
        (after1, before1, across(after1), across(before1)),
    )
    facing0, facing1, a0, b0, fa0, fb0, a1, b1, fa1, fb1 = tie(
        (facing0, facing1, a0, b0, fa0, fb0, a1, b1, fa1, fb1)
    )
    f0, ff0, f1, ff1 = experts((facing0, across(facing0)), (facing1, across(facing1)))
    o0, fo0, o1, fo1 = experts((own0, across(own0)), (own1, across(own1)))

    pa1, pb0 = across(fa1), across(fb0)
    to_after, to_before, from_before1, from_after0 = tie(
        (
            along_ring(add(f0, across(ff0)), 1),
            along_ring(add(f1, across(ff1)), -1),
            along_ring(add(a1, pa1), 1),
            along_ring(add(b0, pb0), -1),
        )
    )
    from_before0 = along_ring(add(a0, across(fa0), to_after), 1)
    from_after1 = along_ring(add(b1, across(fb1), to_before), -1)
    totals = [
        add(o0, across(fo0), from_before0, from_after0),
        add(o1, across(fo1), from_before1, from_after1),
    ]
    totals = jnp.concatenate(
        [total.reshape(column_count, 1, capacity, model_width) for total in totals], axis=1
    ).reshape(column_count, per_device * capacity, model_width)
    rows_back = columns(totals).reshape(expert_count * capacity, model_width)
    mixed_out = jnp.einsum("ts,sd->td", weights, rows_back, preferred_element_type=jnp.float32)
    return mixed_out.astype(jnp.bfloat16)


def solution(mesh):
    return jax.shard_map(
        body,
        mesh=mesh,
        in_specs=(
            P(("dp", "expert"), None),
            P(("dp", "expert"), None),
            P(("dp", "expert"), None),
            P("expert", "dp", None),
            P("expert", "dp", None),
            P("expert", "dp", None),
        ),
        out_specs=P(("dp", "expert"), None),
        check_vma=False,
    )
```

```python
import functools

import jax
import jax.numpy as jnp
from jax import lax
from jax.experimental import pallas as pl
from jax.experimental.pallas import tpu as pltpu
from jax.sharding import PartitionSpec as P


def expert_kernel(count, *refs):
    pieces, (gate_ref, up_ref, down_ref), outs = refs[:count], refs[count : count + 3], refs[count + 3 :]
    rows = jnp.concatenate([ref[...] for ref in pieces], axis=0)
    transposed = (((1,), (1,)), ((), ()))
    gate_act = lax.dot_general(rows, gate_ref[0], transposed, preferred_element_type=jnp.float32)
    up_act = lax.dot_general(rows, up_ref[0], transposed, preferred_element_type=jnp.float32)
    hidden = (gate_act / (1.0 + jnp.exp(-gate_act)) * up_act).astype(jnp.bfloat16)
    width = down_ref.shape[2]
    step = min(512, width)
    for start in range(0, width, step):
        columns = slice(start, start + step)
        out = jnp.dot(
            hidden, down_ref[0, :, columns], preferred_element_type=jnp.float32
        ).astype(jnp.bfloat16)
        row = 0
        for ref in outs:
            ref[:, columns] = out[row : row + ref.shape[0]]
            row += ref.shape[0]


def expert_rows(pieces, heights, index, gate_weight, up_weight, down_weight):
    width = pieces[0].shape[1]
    height = sum(heights)
    hidden = gate_weight.shape[1]
    count = len(pieces)
    whole = pl.BlockSpec(memory_space=pltpu.VMEM)
    weight = pl.BlockSpec((1, hidden, width), lambda i: (index, 0, 0))
    return pl.pallas_call(
        functools.partial(expert_kernel, count),
        grid=(1,),
        in_specs=[whole] * count + [weight] * 3,
        out_specs=[whole] * len(heights),
        out_shape=[pltpu.VMEM((part, width), jnp.bfloat16) for part in heights],
        cost_estimate=pl.CostEstimate(
            flops=6 * height * hidden * width,
            bytes_accessed=6 * hidden * width + 4 * height * width,
            transcendentals=height * hidden,
        ),
        compiler_params=pltpu.CompilerParams(vmem_limit_bytes=24 * 1024 * 1024),
    )(
        *(pltpu.with_memory_space_constraint(piece, pltpu.VMEM) for piece in pieces),
        *(
            pltpu.with_memory_space_constraint(value, pltpu.HBM)
            for value in (gate_weight, up_weight, down_weight)
        ),
    )


def body(tokens, gate_values, expert_ids, gate_weight, up_weight, down_weight):
    dp_count = lax.axis_size("dp")
    ring = dp_count // 2
    assert ring == 4 and gate_weight.shape[0] == 2
    column_count = lax.axis_size("expert")
    per_device = gate_weight.shape[0]
    expert_count = per_device * column_count
    token_rows, model_width = tokens.shape
    top_count = expert_ids.shape[1]
    capacity = max(2, (5 * token_rows * top_count + 4 * expert_count - 1) // (4 * expert_count))
    chunk_rows = column_count * capacity

    def along_ring(value, step):
        return lax.ppermute(
            value,
            "dp",
            [(2 * y + c, 2 * ((y + step) % ring) + c) for y in range(ring) for c in range(2)],
        )

    def across(value):
        return lax.ppermute(
            value, "dp", [(2 * y + c, 2 * y + 1 - c) for y in range(ring) for c in range(2)]
        )

    slots = expert_count * capacity
    slot = jnp.arange(slots, dtype=jnp.int32)
    chose = expert_ids[:, :, None] == (slot // capacity)[None, None, :]
    hit = jnp.any(chose, axis=1)
    earlier = jnp.arange(token_rows)[None, :] < jnp.arange(token_rows)[:, None]
    ranked = jnp.sum((earlier[:, :, None] & hit[None, :, :]).astype(jnp.int32), axis=1)
    taken = hit & (ranked == (slot % capacity)[None, :])
    chosen = taken.astype(jnp.bfloat16)
    chosen = chosen.reshape(token_rows, column_count, per_device, capacity)
    sent0, sent1 = lax.optimization_barrier(
        tuple(
            jnp.einsum(
                "tcr,td->crd", chosen[:, :, index], tokens, preferred_element_type=jnp.float32
            ).astype(jnp.bfloat16)
            for index in range(2)
        )
    )

    def columns(value):
        return lax.all_to_all(value, "expert", split_axis=0, concat_axis=0, tiled=True)

    def add(*values):
        total = values[0].astype(jnp.float32)
        for value in values[1:]:
            total = total + value.astype(jnp.float32)
        return total.astype(jnp.bfloat16)

    tie = lax.optimization_barrier

    def after_all(value, *others):
        return tie((value, *others))[0]

    n = chunk_rows
    half = n // 2

    def facing(before, after):
        return along_ring(before[:half], 1), along_ring(after[half:], -1)

    def experts(index, own, after, before, low, high):
        near = [own, after, before, low, high]
        far = [across(piece) for piece in (low, high, own, after, before)]
        return expert_rows(
            near + far, (4 * n, n, 3 * n), index, gate_weight, up_weight, down_weight
        )

    mine, for_after, for_before = (slice(k * n, (k + 1) * n) for k in range(3))
    low, high = slice(0, half), slice(half, n)

    def outward(kept, paired):
        kept = kept[3 * n :]
        return (
            along_ring(add(kept[low], paired[low]), 1),
            along_ring(add(kept[high], paired[high]), -1),
        )

    def homeward(kept, paired, to_after, to_before):
        to_after = jnp.pad(to_after.astype(jnp.float32), ((0, half), (0, 0)))
        to_before = jnp.pad(to_before.astype(jnp.float32), ((half, 0), (0, 0)))
        return (
            along_ring(add(kept[for_after], paired[for_after], to_after), 1),
            along_ring(add(kept[for_before], paired[for_before], to_before), -1),
        )

    def returned(kept, paired, home, *others):
        total = add(kept[mine], paired[mine], *home)
        if others:
            total = after_all(total, *others)
        return columns(total.reshape(column_count, capacity, model_width))

    arrived0 = columns(sent0)
    own0 = arrived0.reshape(n, model_width)
    before0, after0 = along_ring(own0, 1), along_ring(own0, -1)
    own1 = columns(after_all(sent1, arrived0)).reshape(n, model_width)
    facing0 = facing(before0, after0)

    before1, after1 = along_ring(own1, 1), along_ring(own1, -1)
    kept0, outer0, inner0 = experts(0, own0, after0, before0, *facing0)
    before1, after1, kept0, outer0, inner0 = tie((before1, after1, kept0, outer0, inner0))
    facing1 = facing(before1, after1)
    out0 = outward(kept0, across(outer0))
    inner0 = across(inner0)
    facing1, out0 = tie((facing1, out0))
    home0 = homeward(kept0, inner0, *out0)
    kept1, outer1, inner1 = experts(1, own1, after1, before1, *facing1)
    home0, kept1, outer1, inner1 = tie((home0, kept1, outer1, inner1))
    out1 = outward(kept1, across(outer1))
    inner1 = across(inner1)
    back0 = returned(kept0, inner0, home0)
    home1 = homeward(kept1, inner1, *out1)
    back1 = returned(kept1, inner1, home1, back0)

    chose, taken, gate_values = after_all((chose, taken, gate_values), home0)
    gates = jnp.sum(jnp.where(chose, gate_values.astype(jnp.float32)[:, :, None], 0.0), axis=1)
    weights = jnp.where(taken, gates, 0.0).astype(jnp.bfloat16)
    weights = weights.reshape(token_rows, column_count, per_device, capacity)
    mixed_out = jnp.zeros((token_rows, model_width), jnp.float32)
    for index, back in enumerate((back0, back1)):
        mixed_out = mixed_out + jnp.einsum(
            "tcr,crd->td", weights[:, :, index], back, preferred_element_type=jnp.float32
        )
    return mixed_out.astype(jnp.bfloat16)


def solution(mesh):
    return jax.shard_map(
        body,
        mesh=mesh,
        in_specs=(
            P(("dp", "expert"), None),
            P(("dp", "expert"), None),
            P(("dp", "expert"), None),
            P("expert", "dp", None),
            P("expert", "dp", None),
            P("expert", "dp", None),
        ),
        out_specs=P(("dp", "expert"), None),
        check_vma=False,
    )
```

```python
import functools

import jax
import jax.numpy as jnp
from jax import lax
from jax.experimental import pallas as pl
from jax.experimental.pallas import tpu as pltpu
from jax.sharding import PartitionSpec as P


def expert_kernel(count, *refs):
    pieces, (gate_ref, up_ref, down_ref), outs = refs[:count], refs[count : count + 3], refs[count + 3 :]
    rows = jnp.concatenate([ref[...] for ref in pieces], axis=0)
    transposed = (((1,), (1,)), ((), ()))
    gate_act = lax.dot_general(rows, gate_ref[0], transposed, preferred_element_type=jnp.float32)
    up_act = lax.dot_general(rows, up_ref[0], transposed, preferred_element_type=jnp.float32)
    hidden = (gate_act / (1.0 + jnp.exp(-gate_act)) * up_act).astype(jnp.bfloat16)
    width = down_ref.shape[2]
    step = min(512, width)
    for start in range(0, width, step):
        columns = slice(start, start + step)
        out = jnp.dot(
            hidden, down_ref[0, :, columns], preferred_element_type=jnp.float32
        ).astype(jnp.bfloat16)
        row = 0
        for ref in outs:
            ref[:, columns] = out[row : row + ref.shape[0]]
            row += ref.shape[0]


def expert_rows(pieces, heights, index, gate_weight, up_weight, down_weight):
    width = pieces[0].shape[1]
    height = sum(heights)
    hidden = gate_weight.shape[1]
    count = len(pieces)
    whole = pl.BlockSpec(memory_space=pltpu.VMEM)
    weight = pl.BlockSpec((1, hidden, width), lambda i: (index, 0, 0))
    return pl.pallas_call(
        functools.partial(expert_kernel, count),
        grid=(1,),
        in_specs=[whole] * count + [weight] * 3,
        out_specs=[whole] * len(heights),
        out_shape=[pltpu.VMEM((part, width), jnp.bfloat16) for part in heights],
        cost_estimate=pl.CostEstimate(
            flops=6 * height * hidden * width,
            bytes_accessed=6 * hidden * width + 4 * height * width,
            transcendentals=height * hidden,
        ),
        compiler_params=pltpu.CompilerParams(vmem_limit_bytes=24 * 1024 * 1024),
    )(
        *(pltpu.with_memory_space_constraint(piece, pltpu.VMEM) for piece in pieces),
        *(
            pltpu.with_memory_space_constraint(value, pltpu.HBM)
            for value in (gate_weight, up_weight, down_weight)
        ),
    )


def body(tokens, gate_values, expert_ids, gate_weight, up_weight, down_weight):
    dp_count = lax.axis_size("dp")
    ring = dp_count // 2
    assert ring == 4 and gate_weight.shape[0] == 2
    column_count = lax.axis_size("expert")
    per_device = gate_weight.shape[0]
    expert_count = per_device * column_count
    token_rows, model_width = tokens.shape
    top_count = expert_ids.shape[1]
    capacity = max(2, (5 * token_rows * top_count + 4 * expert_count - 1) // (4 * expert_count))
    chunk_rows = column_count * capacity

    def along_ring(value, step):
        return lax.ppermute(
            value,
            "dp",
            [(2 * y + c, 2 * ((y + step) % ring) + c) for y in range(ring) for c in range(2)],
        )

    def across(value):
        return lax.ppermute(
            value, "dp", [(2 * y + c, 2 * y + 1 - c) for y in range(ring) for c in range(2)]
        )

    slots = expert_count * capacity
    slot = jnp.arange(slots, dtype=jnp.int32)
    chose = expert_ids[:, :, None] == (slot // capacity)[None, None, :]
    hit = jnp.any(chose, axis=1)
    earlier = jnp.arange(token_rows)[None, :] < jnp.arange(token_rows)[:, None]
    ranked = jnp.sum((earlier[:, :, None] & hit[None, :, :]).astype(jnp.int32), axis=1)
    taken = hit & (ranked == (slot % capacity)[None, :])
    chosen = taken.astype(jnp.bfloat16)
    chosen = chosen.reshape(token_rows, column_count, per_device, capacity)
    sent0, sent1 = lax.optimization_barrier(
        tuple(
            jnp.einsum(
                "tcr,td->crd", chosen[:, :, index], tokens, preferred_element_type=jnp.float32
            ).astype(jnp.bfloat16)
            for index in range(2)
        )
    )

    def columns(value):
        return lax.all_to_all(value, "expert", split_axis=0, concat_axis=0, tiled=True)

    def add(*values):
        total = values[0].astype(jnp.float32)
        for value in values[1:]:
            total = total + value.astype(jnp.float32)
        return total.astype(jnp.bfloat16)

    tie = lax.optimization_barrier

    def after_all(value, *others):
        return tie((value, *others))[0]

    n = chunk_rows
    half = n // 2

    def facing(before, after):
        return along_ring(before[:half], 1), along_ring(after[half:], -1)

    def experts(index, own, after, before, low, high):
        near = [own, after, before, low, high]
        far = [across(piece) for piece in (low, high, own, after, before)]
        return expert_rows(
            near + far, (4 * n, n, 3 * n), index, gate_weight, up_weight, down_weight
        )

    mine, for_after, for_before = (slice(k * n, (k + 1) * n) for k in range(3))
    low, high = slice(0, half), slice(half, n)

    def outward(kept, paired):
        kept = kept[3 * n :]
        return (
            along_ring(add(kept[low], paired[low]), 1),
            along_ring(add(kept[high], paired[high]), -1),
        )

    def homeward(kept, paired, to_after, to_before):
        to_after = jnp.pad(to_after.astype(jnp.float32), ((0, half), (0, 0)))
        to_before = jnp.pad(to_before.astype(jnp.float32), ((half, 0), (0, 0)))
        return (
            along_ring(add(kept[for_after], paired[for_after], to_after), 1),
            along_ring(add(kept[for_before], paired[for_before], to_before), -1),
        )

    def returned(kept, paired, home, *others):
        total = add(kept[mine], paired[mine], *home)
        if others:
            total = after_all(total, *others)
        return columns(total.reshape(column_count, capacity, model_width))

    arrived0 = columns(sent0)
    own0 = arrived0.reshape(n, model_width)
    before0, after0 = along_ring(own0, 1), along_ring(own0, -1)
    own1 = columns(after_all(sent1, arrived0)).reshape(n, model_width)
    facing0 = facing(before0, after0)

    before1, after1 = along_ring(own1, 1), along_ring(own1, -1)
    kept0, outer0, inner0 = experts(0, own0, after0, before0, *facing0)
    outer0, inner0 = across(outer0), across(inner0)
    before1, after1, kept0 = tie((before1, after1, kept0))
    facing1 = facing(before1, after1)
    out0 = outward(kept0, outer0)
    facing1, out0 = tie((facing1, out0))
    home0 = homeward(kept0, inner0, *out0)
    kept1, outer1, inner1 = experts(1, own1, after1, before1, *facing1)
    outer1, inner1 = across(outer1), across(inner1)
    home0, kept1 = tie((home0, kept1))
    out1 = outward(kept1, outer1)
    back0 = returned(kept0, inner0, home0)
    home1 = homeward(kept1, inner1, *out1)
    back1 = returned(kept1, inner1, home1, back0)

    chose, taken, gate_values = after_all((chose, taken, gate_values), home0)
    gates = jnp.sum(jnp.where(chose, gate_values.astype(jnp.float32)[:, :, None], 0.0), axis=1)
    weights = jnp.where(taken, gates, 0.0).astype(jnp.bfloat16)
    weights = weights.reshape(token_rows, column_count, per_device, capacity)
    mixed_out = jnp.zeros((token_rows, model_width), jnp.float32)
    for index, back in enumerate((back0, back1)):
        mixed_out = mixed_out + jnp.einsum(
            "tcr,crd->td", weights[:, :, index], back, preferred_element_type=jnp.float32
        )
    return mixed_out.astype(jnp.bfloat16)


def solution(mesh):
    return jax.shard_map(
        body,
        mesh=mesh,
        in_specs=(
            P(("dp", "expert"), None),
            P(("dp", "expert"), None),
            P(("dp", "expert"), None),
            P("expert", "dp", None),
            P("expert", "dp", None),
            P("expert", "dp", None),
        ),
        out_specs=P(("dp", "expert"), None),
        check_vma=False,
    )
```

```python
import functools

import jax
import jax.numpy as jnp
from jax import lax
from jax.experimental import pallas as pl
from jax.experimental.pallas import tpu as pltpu
from jax.sharding import PartitionSpec as P


def expert_kernel(count, *refs):
    pieces, (gate_ref, up_ref, down_ref), outs = refs[:count], refs[count : count + 3], refs[count + 3 :]
    rows = jnp.concatenate([ref[...] for ref in pieces], axis=0)
    transposed = (((1,), (1,)), ((), ()))
    gate_act = lax.dot_general(rows, gate_ref[0], transposed, preferred_element_type=jnp.float32)
    up_act = lax.dot_general(rows, up_ref[0], transposed, preferred_element_type=jnp.float32)
    hidden = (gate_act / (1.0 + jnp.exp(-gate_act)) * up_act).astype(jnp.bfloat16)
    width = down_ref.shape[2]
    step = min(512, width)
    for start in range(0, width, step):
        columns = slice(start, start + step)
        out = jnp.dot(
            hidden, down_ref[0, :, columns], preferred_element_type=jnp.float32
        ).astype(jnp.bfloat16)
        row = 0
        for ref in outs:
            ref[:, columns] = out[row : row + ref.shape[0]]
            row += ref.shape[0]


def expert_rows(pieces, heights, index, gate_weight, up_weight, down_weight):
    width = pieces[0].shape[1]
    height = sum(heights)
    hidden = gate_weight.shape[1]
    count = len(pieces)
    whole = pl.BlockSpec(memory_space=pltpu.VMEM)
    weight = pl.BlockSpec((1, hidden, width), lambda i: (index, 0, 0))
    return pl.pallas_call(
        functools.partial(expert_kernel, count),
        grid=(1,),
        in_specs=[whole] * count + [weight] * 3,
        out_specs=[whole] * len(heights),
        out_shape=[pltpu.VMEM((part, width), jnp.bfloat16) for part in heights],
        cost_estimate=pl.CostEstimate(
            flops=6 * height * hidden * width,
            bytes_accessed=6 * hidden * width + 4 * height * width,
            transcendentals=height * hidden,
        ),
        compiler_params=pltpu.CompilerParams(vmem_limit_bytes=24 * 1024 * 1024),
    )(
        *(pltpu.with_memory_space_constraint(piece, pltpu.VMEM) for piece in pieces),
        *(
            pltpu.with_memory_space_constraint(value, pltpu.HBM)
            for value in (gate_weight, up_weight, down_weight)
        ),
    )


def body(tokens, gate_values, expert_ids, gate_weight, up_weight, down_weight):
    dp_count = lax.axis_size("dp")
    ring = dp_count // 2
    assert ring == 4 and gate_weight.shape[0] == 2
    column_count = lax.axis_size("expert")
    per_device = gate_weight.shape[0]
    expert_count = per_device * column_count
    token_rows, model_width = tokens.shape
    top_count = expert_ids.shape[1]
    capacity = max(2, (5 * token_rows * top_count + 4 * expert_count - 1) // (4 * expert_count))
    chunk_rows = column_count * capacity

    def along_ring(value, step):
        return lax.ppermute(
            value,
            "dp",
            [(2 * y + c, 2 * ((y + step) % ring) + c) for y in range(ring) for c in range(2)],
        )

    def across(value):
        return lax.ppermute(
            value, "dp", [(2 * y + c, 2 * y + 1 - c) for y in range(ring) for c in range(2)]
        )

    slots = expert_count * capacity
    slot = jnp.arange(slots, dtype=jnp.int32)
    chose = expert_ids[:, :, None] == (slot // capacity)[None, None, :]
    hit = jnp.any(chose, axis=1)
    earlier = jnp.arange(token_rows)[None, :] < jnp.arange(token_rows)[:, None]
    ranked = jnp.sum((earlier[:, :, None] & hit[None, :, :]).astype(jnp.int32), axis=1)
    taken = hit & (ranked == (slot % capacity)[None, :])
    chosen = taken.astype(jnp.bfloat16)
    chosen = chosen.reshape(token_rows, column_count, per_device, capacity)
    sent0, sent1 = lax.optimization_barrier(
        tuple(
            jnp.einsum(
                "ts,td->sd",
                chosen[:, :, index].reshape(token_rows, chunk_rows),
                tokens,
                preferred_element_type=jnp.float32,
            )
            .astype(jnp.bfloat16)
            .reshape(column_count, capacity, model_width)
            for index in range(2)
        )
    )

    def columns(value):
        return lax.all_to_all(value, "expert", split_axis=0, concat_axis=0, tiled=True)

    def add(*values):
        total = values[0].astype(jnp.float32)
        for value in values[1:]:
            total = total + value.astype(jnp.float32)
        return total.astype(jnp.bfloat16)

    tie = lax.optimization_barrier

    def after_all(value, *others):
        return tie((value, *others))[0]

    n = chunk_rows
    half = n // 2

    def facing(before, after):
        return along_ring(before[:half], 1), along_ring(after[half:], -1)

    def experts(index, own, after, before, low, high):
        near = [own, after, before, low, high]
        far = [across(piece) for piece in (low, high, own, after, before)]
        return expert_rows(
            near + far, (4 * n, n, 3 * n), index, gate_weight, up_weight, down_weight
        )

    mine, for_after, for_before = (slice(k * n, (k + 1) * n) for k in range(3))
    low, high = slice(0, half), slice(half, n)

    def outward(kept, paired):
        kept = kept[3 * n :]
        return (
            along_ring(add(kept[low], paired[low]), 1),
            along_ring(add(kept[high], paired[high]), -1),
        )

    def homeward(kept, paired, to_after, to_before):
        to_after = jnp.pad(to_after.astype(jnp.float32), ((0, half), (0, 0)))
        to_before = jnp.pad(to_before.astype(jnp.float32), ((half, 0), (0, 0)))
        return (
            along_ring(add(kept[for_after], paired[for_after], to_after), 1),
            along_ring(add(kept[for_before], paired[for_before], to_before), -1),
        )

    def returned(kept, paired, home, *others):
        total = add(kept[mine], paired[mine], *home).reshape(column_count, capacity, model_width)
        if others:
            total = after_all(total, *others)
        return columns(total)

    arrived0 = columns(sent0)
    own0 = arrived0.reshape(n, model_width)
    before0, after0 = along_ring(own0, 1), along_ring(own0, -1)
    own1 = columns(after_all(sent1, arrived0)).reshape(n, model_width)
    facing0 = facing(before0, after0)

    before1, after1 = along_ring(own1, 1), along_ring(own1, -1)
    kept0, outer0, inner0 = experts(0, own0, after0, before0, *facing0)
    outer0, inner0 = across(outer0), across(inner0)
    before1, after1, kept0 = tie((before1, after1, kept0))
    facing1 = facing(before1, after1)
    out0 = outward(kept0, outer0)
    facing1, out0 = tie((facing1, out0))
    home0 = homeward(kept0, inner0, *out0)
    kept1, outer1, inner1 = experts(1, own1, after1, before1, *facing1)
    outer1, inner1 = across(outer1), across(inner1)
    home0, kept1 = tie((home0, kept1))
    out1 = outward(kept1, outer1)
    chose, taken, gate_values = after_all((chose, taken, gate_values), out0)
    gates = jnp.sum(jnp.where(chose, gate_values.astype(jnp.float32)[:, :, None], 0.0), axis=1)
    weights = jnp.where(taken, gates, 0.0).astype(jnp.bfloat16)
    weights = weights.reshape(token_rows, column_count, per_device, capacity)

    def weighted(index, back):
        return jnp.einsum(
            "ts,sd->td",
            weights[:, :, index].reshape(token_rows, chunk_rows),
            back.reshape(chunk_rows, model_width),
            preferred_element_type=jnp.float32,
        )

    mixed0 = weighted(0, returned(kept0, inner0, home0))
    home1 = homeward(kept1, inner1, *out1)
    mixed1 = weighted(1, returned(kept1, inner1, home1, mixed0))
    return (mixed0 + mixed1).astype(jnp.bfloat16)


def solution(mesh):
    return jax.shard_map(
        body,
        mesh=mesh,
        in_specs=(
            P(("dp", "expert"), None),
            P(("dp", "expert"), None),
            P(("dp", "expert"), None),
            P("expert", "dp", None),
            P("expert", "dp", None),
            P("expert", "dp", None),
        ),
        out_specs=P(("dp", "expert"), None),
        check_vma=False,
    )
```

```python
import functools

import jax
import jax.numpy as jnp
from jax import lax
from jax.experimental import pallas as pl
from jax.experimental.pallas import tpu as pltpu
from jax.sharding import PartitionSpec as P


def expert_kernel(count, *refs):
    pieces, (gate_ref, up_ref, down_ref), outs = refs[:count], refs[count : count + 3], refs[count + 3 :]
    rows = jnp.concatenate([ref[...] for ref in pieces], axis=0)
    transposed = (((1,), (1,)), ((), ()))
    gate_act = lax.dot_general(rows, gate_ref[0], transposed, preferred_element_type=jnp.float32)
    up_act = lax.dot_general(rows, up_ref[0], transposed, preferred_element_type=jnp.float32)
    hidden = (gate_act / (1.0 + jnp.exp(-gate_act)) * up_act).astype(jnp.bfloat16)
    width = down_ref.shape[2]
    step = min(512, width)
    for start in range(0, width, step):
        columns = slice(start, start + step)
        out = jnp.dot(
            hidden, down_ref[0, :, columns], preferred_element_type=jnp.float32
        ).astype(jnp.bfloat16)
        row = 0
        for ref in outs:
            ref[:, columns] = out[row : row + ref.shape[0]]
            row += ref.shape[0]


def expert_rows(pieces, heights, index, gate_weight, up_weight, down_weight):
    width = pieces[0].shape[1]
    height = sum(heights)
    hidden = gate_weight.shape[1]
    count = len(pieces)
    whole = pl.BlockSpec(memory_space=pltpu.VMEM)
    weight = pl.BlockSpec(
        (1, hidden, width), lambda i: (index, 0, 0), pipeline_mode=pl.Buffered(1)
    )
    return pl.pallas_call(
        functools.partial(expert_kernel, count),
        grid=(1,),
        in_specs=[whole] * count + [weight] * 3,
        out_specs=[whole] * len(heights),
        out_shape=[pltpu.VMEM((part, width), jnp.bfloat16) for part in heights],
        cost_estimate=pl.CostEstimate(
            flops=6 * height * hidden * width,
            bytes_accessed=6 * hidden * width + 4 * height * width,
            transcendentals=height * hidden,
        ),
        compiler_params=pltpu.CompilerParams(vmem_limit_bytes=15 * 1024 * 1024),
    )(
        *(pltpu.with_memory_space_constraint(piece, pltpu.VMEM) for piece in pieces),
        *(
            pltpu.with_memory_space_constraint(value, pltpu.HBM)
            for value in (gate_weight, up_weight, down_weight)
        ),
    )


def body(tokens, gate_values, expert_ids, gate_weight, up_weight, down_weight):
    dp_count = lax.axis_size("dp")
    ring = dp_count // 2
    assert ring == 4 and gate_weight.shape[0] == 2
    column_count = lax.axis_size("expert")
    per_device = gate_weight.shape[0]
    expert_count = per_device * column_count
    token_rows, model_width = tokens.shape
    top_count = expert_ids.shape[1]
    capacity = max(2, (5 * token_rows * top_count + 4 * expert_count - 1) // (4 * expert_count))
    chunk_rows = column_count * capacity

    def along_ring(value, step):
        return lax.ppermute(
            value,
            "dp",
            [(2 * y + c, 2 * ((y + step) % ring) + c) for y in range(ring) for c in range(2)],
        )

    def across(value):
        return lax.ppermute(
            value, "dp", [(2 * y + c, 2 * y + 1 - c) for y in range(ring) for c in range(2)]
        )

    slots = expert_count * capacity
    slot = jnp.arange(slots, dtype=jnp.int32)
    chose = expert_ids[:, :, None] == (slot // capacity)[None, None, :]
    hit = jnp.any(chose, axis=1)
    earlier = jnp.arange(token_rows)[None, :] < jnp.arange(token_rows)[:, None]
    ranked = jnp.sum((earlier[:, :, None] & hit[None, :, :]).astype(jnp.int32), axis=1)
    taken = hit & (ranked == (slot % capacity)[None, :])
    chosen = taken.astype(jnp.bfloat16)
    chosen = chosen.reshape(token_rows, column_count, per_device, capacity)
    sent0, sent1 = (
        jnp.einsum(
            "ts,td->sd",
            chosen[:, :, index].reshape(token_rows, chunk_rows),
            tokens,
            preferred_element_type=jnp.float32,
        )
        .astype(jnp.bfloat16)
        .reshape(column_count, capacity, model_width)
        for index in range(2)
    )

    def columns(value):
        return lax.all_to_all(value, "expert", split_axis=0, concat_axis=0, tiled=True)

    def add(*values):
        total = values[0].astype(jnp.float32)
        for value in values[1:]:
            total = total + value.astype(jnp.float32)
        return total.astype(jnp.bfloat16)

    tie = lax.optimization_barrier

    def after_all(value, *others):
        return tie((value, *others))[0]

    n = chunk_rows
    half = n // 2

    def facing(before, after):
        return along_ring(before[:half], 1), along_ring(after[half:], -1)

    def experts(index, own, after, before, low, high):
        near = [own, after, before, low, high]
        far = [across(piece) for piece in (low, high, own, after, before)]
        return expert_rows(
            near + far, (4 * n, n, 3 * n), index, gate_weight, up_weight, down_weight
        )

    mine, for_after, for_before = (slice(k * n, (k + 1) * n) for k in range(3))
    low, high = slice(0, half), slice(half, n)

    def outward(kept, paired):
        kept = kept[3 * n :]
        return (
            along_ring(add(kept[low], paired[low]), 1),
            along_ring(add(kept[high], paired[high]), -1),
        )

    def homeward(kept, paired, to_after, to_before):
        to_after = jnp.pad(to_after.astype(jnp.float32), ((0, half), (0, 0)))
        to_before = jnp.pad(to_before.astype(jnp.float32), ((half, 0), (0, 0)))
        return (
            along_ring(add(kept[for_after], paired[for_after], to_after), 1),
            along_ring(add(kept[for_before], paired[for_before], to_before), -1),
        )

    def returned(kept, paired, home, *others):
        total = add(kept[mine], paired[mine], *home).reshape(column_count, capacity, model_width)
        if others:
            total = after_all(total, *others)
        return columns(total)

    arrived0, sent1 = tie((columns(sent0), sent1))
    own0 = arrived0.reshape(n, model_width)
    before0, after0 = along_ring(own0, 1), along_ring(own0, -1)
    own1 = columns(sent1).reshape(n, model_width)
    facing0 = facing(before0, after0)

    before1, after1 = along_ring(own1, 1), along_ring(own1, -1)
    kept0, outer0, inner0 = experts(0, own0, after0, before0, *facing0)
    outer0, inner0 = across(outer0), across(inner0)
    before1, after1, kept0 = tie((before1, after1, kept0))
    facing1 = facing(before1, after1)
    out0 = outward(kept0, outer0)
    facing1, out0 = tie((facing1, out0))
    home0 = homeward(kept0, inner0, *out0)
    kept1, outer1, inner1 = experts(1, own1, after1, before1, *facing1)
    outer1, inner1 = across(outer1), across(inner1)
    home0, kept1 = tie((home0, kept1))
    out1 = outward(kept1, outer1)
    chose, taken, gate_values = after_all((chose, taken, gate_values), out0)
    gates = jnp.sum(jnp.where(chose, gate_values.astype(jnp.float32)[:, :, None], 0.0), axis=1)
    weights = jnp.where(taken, gates, 0.0).astype(jnp.bfloat16)
    weights = weights.reshape(token_rows, column_count, per_device, capacity)

    def weighted(index, back):
        return jnp.einsum(
            "ts,sd->td",
            weights[:, :, index].reshape(token_rows, chunk_rows),
            back.reshape(chunk_rows, model_width),
            preferred_element_type=jnp.float32,
        )

    mixed0 = weighted(0, returned(kept0, inner0, home0))
    home1 = homeward(kept1, inner1, *out1)
    mixed1 = weighted(1, returned(kept1, inner1, home1, mixed0))
    return (mixed0 + mixed1).astype(jnp.bfloat16)


def solution(mesh):
    return jax.shard_map(
        body,
        mesh=mesh,
        in_specs=(
            P(("dp", "expert"), None),
            P(("dp", "expert"), None),
            P(("dp", "expert"), None),
            P("expert", "dp", None),
            P("expert", "dp", None),
            P("expert", "dp", None),
        ),
        out_specs=P(("dp", "expert"), None),
        check_vma=False,
    )
```
